512 devices in a mesh: section: 64 (over z, y_lo, core), tensor: 8 (over x, y_hi).
Axes of the slice: x: 4, y: 4 (y_hi: 2, y_lo: 2; y = y_hi * 2 + y_lo), z: 16, core: 2. Of those that a mesh axis runs over, the one named last changes fastest.
Arguments:
- queries: bfloat16 [24576, 5120], P('section', 'tensor'), may hold values from -6 to 6, as said below
- keys: bfloat16 [24576, 5120], P('section', 'tensor'), may hold values from -6 to 6, as said below
- values: bfloat16 [24576, 5120], P('section', 'tensor'), may hold values from -12 to 12
- q_gain: float32 [5120], P('tensor'), may hold values from 1 to 2.5
- k_gain: float32 [5120], P('tensor'), may hold values from 1 to 2.5
- frame_offset: int32 [64], P('section'), may hold values from 0 to 255, as said below
- noise_level: int32 [64], P('section'), may hold values from 0 to 127, as said below
- gate_table: float32 [128, 5120], P(None, 'tensor'), may hold values from -6 to 6
- out_weight: bfloat16 [5120, 5120], P('tensor', 'section'), may hold values from -0.078125 to 0.078125
- latent: bfloat16 [24576, 5120], P('section', 'tensor'), may hold values from -6 to 6
- fresh: bfloat16 [384, 5120], P(None, 'tensor'), may hold values from -6 to 6
Outputs:
- queue_next: bfloat16 [24576, 5120], P('section', 'tensor')
The draws below stay inside these ranges and needn't reach their ends.
Inputs may be any that keep to these rules, and one draw needn't show every extreme that they name: `queries`: entries are real values; rows are not normalized. `keys`: entries are real values; rows are not normalized. `frame_offset`: frame 0 has offset 0, the last frame 4 * 64 - 1, and offsets rise by 1 to 7 from each frame to the next. `noise_level`: frame 0 has level 0, the last frame 128 - 1, and levels rise by 1 to 3 from each frame to the next.
All inputs are finite; a program needn't handle non-finite values.
Results may differ from the reference program's by a relative error of at most 0.013.
Values may be sent and summed in bfloat16 or wider, within the bound.
A program may use at most 64 MiB of HBM per device.

```python
import math
import jax
import jax.numpy as jnp
from jax import lax

D = 5120
HD = 128
TOK_DEV = 384
SPANS = 64
ROWS = 24576
LEVELS = 128
N_TENSOR = 8


def draw_queries(key, part):
    key = jax.random.fold_in(key, 5)
    result = jnp.clip(jax.random.normal(key, (ROWS, D), jnp.float32), -6.0, 6.0)
    return result.astype(jnp.bfloat16)


def draw_keys(key, part):
    key = jax.random.fold_in(key, 7)
    result = jnp.clip(jax.random.normal(key, (ROWS, D), jnp.float32), -6.0, 6.0)
    return result.astype(jnp.bfloat16)


def draw_frame_offset(key, part):
    key = jax.random.fold_in(key, 21)
    jitter = jax.random.randint(key, (SPANS,), 0, 4)
    place = jnp.arange(SPANS, dtype=jnp.int32)
    jitter = jnp.where(place == 0, 0, jnp.where(place == SPANS - 1, 3, jitter))
    return (4 * place + jitter).astype(jnp.int32)


def draw_noise_level(key, part):
    key = jax.random.fold_in(key, 31)
    jitter = jax.random.randint(key, (SPANS,), 0, 2)
    place = jnp.arange(SPANS, dtype=jnp.int32)
    jitter = jnp.where(place == 0, 0, jnp.where(place == SPANS - 1, 1, jitter))
    return (2 * place + jitter).astype(jnp.int32)


def shard_levels(own_key, extent, cuts, smallest, largest):
    level, own = 1.0, jax.random.fold_in(own_key, 6)
    for position, shards_of in cuts:
        heights = jnp.exp(jax.random.uniform(jax.random.fold_in(own, position), (shards_of,), jnp.float32, smallest / len(cuts), largest / len(cuts)))
        level = level * jnp.repeat(heights, extent[position] // shards_of).reshape([-1 if axis == position else 1 for axis in range(len(extent))])
    return level


def bell_draw(rng, shape, deviation, most, cuts=(), kind=jnp.bfloat16):
    level = shard_levels(rng, shape, cuts, -0.22, 0.18) if cuts else 1.0
    values = jax.random.normal(rng, shape, jnp.float32) * deviation * level
    return jnp.minimum(jnp.maximum(values, -most), most).astype(kind)


def setup_inputs(seed: int = 0) -> dict:
    seeds = jax.random.split(jax.random.key(seed), 12)
    return {
        "queries": draw_queries(jax.random.fold_in(seeds[11], 71), 0),
        "keys": draw_keys(jax.random.fold_in(seeds[11], 71), 0),
        "values": bell_draw(seeds[2], (ROWS, D), 2.0, 12.0, ((0, 64), (1, 8))),
        "q_gain": jnp.clip(jnp.exp(math.log(2.5) - 0.916290732 * jax.random.uniform(seeds[3], (D,), jnp.float32) ** shard_levels(seeds[3], (D,), ((0, 8),), -0.2, 0.2)), 1.0, 2.5),
        "k_gain": jnp.clip(jnp.exp(math.log(2.5) - 0.916290732 * jax.random.uniform(seeds[4], (D,), jnp.float32) ** shard_levels(seeds[4], (D,), ((0, 8),), -0.2, 0.2)), 1.0, 2.5),
        "frame_offset": draw_frame_offset(jax.random.fold_in(seeds[11], 71), 0),
        "noise_level": draw_noise_level(jax.random.fold_in(seeds[11], 71), 0),
        "gate_table": bell_draw(seeds[7], (LEVELS, D), 1.0, 6.0, ((1, 8),), jnp.float32),
        "out_weight": bell_draw(seeds[8], (D, D), D ** -0.5, 0.078125, ((0, 8), (1, 64))),
        "latent": bell_draw(seeds[9], (ROWS, D), 1.0, 6.0, ((0, 64), (1, 8))),
        "fresh": bell_draw(seeds[10], (TOK_DEV, D), 1.0, 6.0, ((1, 8),)),
    }


EPSILON = 1e-06

def normalize(inputs, gain):
    widened = inputs.astype(jnp.float32)
    mean_square = lax.optimization_barrier(jnp.mean(widened * widened, axis=-1, keepdims=True))
    return widened * lax.rsqrt(mean_square + EPSILON) * gain

def rotate(inputs, offsets):
    half_width = HD // 2
    pair_index = jnp.arange(half_width, dtype=jnp.float32)
    pair_rate = jnp.exp(pair_index * (-math.log(10000.0) / half_width))
    angles = offsets.astype(jnp.float32)[:, None, None] * pair_rate
    row_count = inputs.shape[0]
    by_head = inputs.reshape(row_count, -1, HD)
    leading = by_head[..., :half_width]
    trailing = by_head[..., half_width:]
    cosines = jnp.cos(angles)
    sine_part = jnp.sin(angles)
    turned = jnp.concatenate([leading * cosines - trailing * sine_part, leading * sine_part + trailing * cosines], axis=-1)
    return turned.reshape(row_count, -1)

def attend(q_block, k_block, v_block, usable):
    tokens = q_block.shape[0]
    q_heads = q_block.reshape(tokens, -1, HD).astype(jnp.float32)
    k_heads = k_block.reshape(k_block.shape[0], -1, HD).astype(jnp.float32)
    v_heads = v_block.reshape(v_block.shape[0], -1, HD).astype(jnp.float32)
    scores = jnp.einsum('qhd,khd->hqk', q_heads, k_heads) * (1.0 / math.sqrt(HD))
    scores = jnp.where(usable[None, None, :], scores, -jnp.inf)
    highest = lax.optimization_barrier(jnp.max(scores, axis=-1, keepdims=True))
    raised = jnp.exp(scores - highest)
    weights = (raised / lax.optimization_barrier(jnp.sum(raised, axis=-1, keepdims=True))).astype(jnp.bfloat16)
    mixed = jnp.einsum('hqk,khd->qhd', weights.astype(jnp.float32), v_heads)
    return mixed.astype(jnp.bfloat16).reshape(tokens, -1)

def reference(queries, keys, values, q_gain, k_gain, frame_offset, noise_level, gate_table, out_weight, latent, fresh):
    row_offsets = jnp.repeat(frame_offset, TOK_DEV)
    q_normed = rotate(normalize(queries, q_gain), row_offsets).astype(jnp.bfloat16)
    k_normed = rotate(normalize(keys, k_gain), row_offsets).astype(jnp.bfloat16)
    blank = jnp.zeros((TOK_DEV, D), jnp.bfloat16)
    k_padded = jnp.concatenate([blank, k_normed, blank], axis=0)
    v_padded = jnp.concatenate([blank, values, blank], axis=0)
    group = D // N_TENSOR

    def one_frame(frame):
        start = (frame * TOK_DEV).astype(jnp.int32)
        q_block = lax.dynamic_slice_in_dim(q_normed, start, TOK_DEV, 0)
        k_block = lax.dynamic_slice_in_dim(k_padded, start, 3 * TOK_DEV, 0)
        v_block = lax.dynamic_slice_in_dim(v_padded, start, 3 * TOK_DEV, 0)
        latent_block = lax.dynamic_slice_in_dim(latent, start, TOK_DEV, 0)
        neighbour = jnp.arange(3 * TOK_DEV, dtype=jnp.int32) // TOK_DEV + frame - 1
        usable = (neighbour >= 0) & (neighbour < SPANS)
        mixed = attend(q_block, k_block, v_block, usable)
        projected = jnp.zeros((TOK_DEV, D), jnp.float32)
        for member in range(N_TENSOR):
            partial_sum = jnp.dot(mixed[:, member * group:(member + 1) * group], out_weight[member * group:(member + 1) * group], preferred_element_type=jnp.float32)
            rounded = lax.optimization_barrier(partial_sum.astype(jnp.bfloat16))
            projected = projected + rounded.astype(jnp.float32)
        gate_row = gate_table[noise_level[frame]]
        return (latent_block.astype(jnp.float32) + gate_row * projected).astype(jnp.bfloat16)
    updated = lax.map(one_frame, jnp.arange(SPANS, dtype=jnp.int32))
    moved = updated[:-1].reshape(-1, D)
    return jnp.concatenate([fresh, moved], axis=0)
```

```python
import math

import jax
import jax.numpy as jnp
from jax import lax
from jax.experimental import pallas as pl
from jax.experimental.pallas import tpu as pltpu
from jax.sharding import PartitionSpec as P

D = 5120
HD = 128
EPSILON = 1e-06
TOK = 384
WIDTH = 640
HEADS = WIDTH // HD
SLAB = 80
MASKED = -1e30
COLUMNS = ((0, 256), (256, 256), (512, 128))
NT = (((1,), (1,)), ((), ()))


def dot_nt(a, b):
    return lax.dot_general(a, b, NT, preferred_element_type=jnp.float32)


def dot_nn(a, b):
    return jnp.dot(a, b, preferred_element_type=jnp.float32)


def kernel(
    q_ref,
    k_ref,
    v_ref,
    table_ref,
    gate_ref,
    latent_ref,
    slab_ref,
    out_ref,
    squares,
    q_n,
    k_all,
    v_all,
    peak,
    total,
    mixed,
    gathered,
    weight,
    acc,
    staged,
    landed,
    gate_prev,
    sq_send,
    sq_recv,
    halo_send,
    halo_recv,
    gate_send,
    gate_recv,
    swap_send,
    swap_recv,
    side_send,
    side_recv,
    ring_send,
    ring_recv,
    twin_send,
    twin_recv,
    a_send,
    a_recv,
    f_send,
    f_recv,
    o_send,
    o_recv,
):
    sec = lax.axis_index("section")
    ten = lax.axis_index("tensor")
    z = lax.div(sec, 4)
    zh = lax.div(sec, 16)
    core = lax.rem(sec, 2)
    yl = lax.rem(lax.div(sec, 2), 2)
    x = lax.div(ten, 2)
    h = lax.rem(ten, 2)
    near = sec + 1 - 2 * core
    far = lax.rem(sec + 2 * core + 63, 64)
    following = lax.rem(sec + 1, 64)
    previous = lax.rem(sec + 63, 64)
    z_next = lax.rem(sec + 4, 64)
    z_last = lax.rem(sec + 60, 64)
    y_side = sec + 2 - 4 * yl
    x_right = lax.rem(x + 1, 4) * 2 + h
    x_left = lax.rem(x + 3, 4) * 2 + h
    other = ten + 1 - 2 * h
    swap_sec = 16 * x + lax.rem(sec, 16)
    swap_ten = 2 * zh + h
    stays = x == zh

    def remote(src, dst, send, recv, section, tensor):
        return pltpu.make_async_remote_copy(
            src_ref=src,
            dst_ref=dst,
            send_sem=send,
            recv_sem=recv,
            device_id={"section": section, "tensor": tensor},
            device_id_type=pl.DeviceIdType.MESH,
        )

    sent = []

    def send(src, dst, send_sem, recv_sem, section, tensor):
        copy = remote(src, dst, send_sem, recv_sem, section, tensor)
        copy.start()
        sent.append(copy)

    def arrived(dst, send_sem, recv_sem):
        remote(dst, dst, send_sem, recv_sem, near, ten).wait_recv()

    barrier = pltpu.get_barrier_semaphore()
    greeted = [(near, ten), (far, ten), (z_next, ten), (z_last, ten), (y_side, ten)]
    greeted += [(following, ten), (following, other), (previous, ten), (previous, other)]
    greeted += [(sec, lax.rem(ten + i, 8)) for i in range(1, 8)]
    for section, tensor in greeted:
        pl.semaphore_signal(
            barrier,
            inc=1,
            device_id={"section": section, "tensor": tensor},
            device_id_type=pl.DeviceIdType.MESH,
        )

    @pl.when(jnp.logical_not(stays))
    def _():
        pl.semaphore_signal(
            barrier,
            inc=1,
            device_id={"section": swap_sec, "tensor": swap_ten},
            device_id_type=pl.DeviceIdType.MESH,
        )

    def lanes(head):
        return slice(head * HD, (head + 1) * HD)

    def row_sums(ref):
        part = jnp.zeros((TOK, HD), jnp.float32)
        for head in range(HEADS):
            wide = ref[:, lanes(head)].astype(jnp.float32)
            part += wide * wide
        return jnp.sum(part.T, axis=0, keepdims=True)

    q_sums, k_sums = row_sums(q_ref), row_sums(k_ref)
    row = lax.broadcasted_iota(jnp.int32, (8, TOK), 0)
    squares[ten] = jnp.where(row < 4, q_sums, k_sums)

    pl.semaphore_wait(barrier, len(greeted) + jnp.where(stays, 0, 1))

    for i in range(1, 8):
        send(
            squares.at[ten], squares.at[ten], sq_send.at[i - 1], sq_recv.at[i - 1], sec,
            lax.rem(ten + i, 8),
        )

    def slab(zz, j, c):
        place = 4 * lax.rem(zz + 16, 16) + 2 * ((1 - yl) if j else yl) + c
        return weight.at[pl.ds(pl.multiple_of(place * SLAB, 16), SLAB)]

    swap = remote(
        slab_ref,
        weight.at[pl.ds(pl.multiple_of(swap_sec * SLAB, 16), SLAB)],
        swap_send,
        swap_recv,
        swap_sec,
        swap_ten,
    )
    keep = pltpu.make_async_copy(slab_ref, slab(z, 0, core), swap_send)

    @pl.when(jnp.logical_not(stays))
    def _():
        swap.start()

    @pl.when(stays)
    def _():
        keep.start()

    mine, by_near, by_far = (pl.ds(i * TOK, TOK) for i in range(3))
    v_near, v_far = v_all.at[pl.ds(0, TOK)], v_all.at[pl.ds(TOK, TOK)]
    send(v_ref, v_far, halo_send.at[0], halo_recv.at[0], far, ten)
    send(v_ref, v_near, halo_send.at[1], halo_recv.at[1], near, ten)
    send(gate_ref, gate_prev, gate_send, gate_recv, following, ten)

    def number(k, j):
        return 14 if k == 8 else 2 * (k - 1) + j

    def origin(d, k):
        return z + k if d else z - k

    def ring(d, k, j):
        n = number(k, j)
        piece = slab(origin(d, k - 1), j, core)
        send(piece, piece, ring_send.at[d, n], ring_recv.at[d, n], z_last if d else z_next, ten)

    def twin(piece, m):
        send(piece, piece, twin_send.at[m], twin_recv.at[m], near, ten)

    def first(j):
        piece = slab(z, j, core)
        for d in range(2):
            ring(d, 1, j)
        twin(piece, j)

    def pump(k):
        for j in range(2):
            for d in range(2):
                if k == 8 and j != d:
                    continue
                n = number(k, j)
                piece = slab(origin(d, k), j, core)
                arrived(piece, ring_send.at[d, n], ring_recv.at[d, n])
                if k < 7 or (k == 7 and j == d):
                    ring(d, k + 1, j)
                twin(piece, 2 + 15 * d + n)

    def twin_arrived(k):
        if k == 0:
            for j in range(2):
                arrived(slab(z, j, 1 - core), twin_send.at[j], twin_recv.at[j])
            return
        for j in range(2):
            for d in range(2):
                if k == 8 and j != d:
                    continue
                m = 2 + 15 * d + number(k, j)
                arrived(slab(origin(d, k), j, 1 - core), twin_send.at[m], twin_recv.at[m])

    @pl.when(jnp.logical_not(stays))
    def _():
        swap.wait_send()
        arrived(slab(z, 0, core), swap_send, swap_recv)

    @pl.when(stays)
    def _():
        keep.wait()

    own_slab = slab(z, 0, core)
    first(0)
    send(own_slab, own_slab, side_send, side_recv, y_side, ten)

    for i in range(1, 8):
        arrived(squares.at[lax.rem(ten + 8 - i, 8)], sq_send.at[i - 1], sq_recv.at[i - 1])
    sums = squares[0]
    for i in range(1, 8):
        sums = sums + squares[i]
    scale = lax.rsqrt(sums / D + EPSILON)
    q_scale = jnp.broadcast_to(scale[0:1], (HD, TOK)).T
    k_scale = jnp.broadcast_to(scale[4:5], (HD, TOK)).T

    def rotated(ref, head, at, by):
        wide = ref[:, lanes(head)].astype(jnp.float32)
        turned = wide * table_ref[at : at + 1, lanes(head)] + pltpu.roll(wide, HD // 2, 1) * (
            table_ref[at + 1 : at + 2, lanes(head)]
        )
        return (turned * by).astype(jnp.bfloat16)

    for head in range(HEADS):
        k_all[mine, lanes(head)] = rotated(k_ref, head, 2, k_scale)
    send(k_all.at[mine], k_all.at[by_far], halo_send.at[2], halo_recv.at[2], far, ten)
    send(k_all.at[mine], k_all.at[by_near], halo_send.at[3], halo_recv.at[3], near, ten)
    for head in range(HEADS):
        q_n[:, lanes(head)] = rotated(q_ref, head, 0, q_scale)

    arrived(slab(z, 1, core), side_send, side_recv)
    first(1)
    pump(1)

    arrived(v_near, halo_send.at[1], halo_recv.at[1])
    arrived(k_all.at[by_near], halo_send.at[3], halo_recv.at[3])
    for head in range(HEADS):
        scores = dot_nt(q_n[:, lanes(head)], k_all[0 : 2 * TOK, lanes(head)])
        highest = jnp.max(scores, axis=-1, keepdims=True)
        raised = jnp.exp2(scores - highest)
        peak[head] = jnp.broadcast_to(highest, (TOK, HD))
        total[head] = jnp.broadcast_to(jnp.sum(raised, axis=-1, keepdims=True), (TOK, HD))
        raised = raised.astype(jnp.bfloat16)
        mixed[head] = dot_nn(raised[:, :TOK], v_ref[:, lanes(head)]) + dot_nn(
            raised[:, TOK:], v_all[0:TOK, lanes(head)]
        )

    pump(2)
    pump(3)

    arrived(v_far, halo_send.at[0], halo_recv.at[0])
    arrived(k_all.at[by_far], halo_send.at[2], halo_recv.at[2])
    absent = jnp.where((sec == 0) | (sec == 63), MASKED, 0.0)

    def pass_on(head):
        for d in range(2):
            source = lax.rem(x + (1 if d else 3), 4)
            here = gathered.at[source, :, lanes(head)]
            arrived(here, a_send.at[d, head], a_recv.at[d, head])
            half = gathered.at[source, pl.ds(d * (TOK // 2), TOK // 2), lanes(head)]
            send(half, half, f_send.at[d, head], f_recv.at[d, head], sec, x_left if d else x_right)

    for head in range(HEADS):
        scores = dot_nt(q_n[:, lanes(head)], k_all[2 * TOK :, lanes(head)]) + absent
        before = peak[head]
        highest = jnp.maximum(before[:, 0:1], jnp.max(scores, axis=-1, keepdims=True))
        raised = jnp.exp2(scores - highest)
        shrink = jnp.exp2(before - highest)
        sums = total[head] * shrink + jnp.sum(raised, axis=-1, keepdims=True)
        result = mixed[head] * shrink + dot_nn(
            raised.astype(jnp.bfloat16), v_all[TOK : 2 * TOK, lanes(head)]
        )
        gathered[x, :, lanes(head)] = (result / sums).astype(jnp.bfloat16)
        own = gathered.at[x, :, lanes(head)]
        for d in range(2):
            send(own, own, a_send.at[d, head], a_recv.at[d, head], sec, x_left if d else x_right)
        if head >= 2:
            pass_on(head - 2)
    pump(4)
    pass_on(HEADS - 2)
    pass_on(HEADS - 1)
    pump(5)
    pump(6)
    pump(7)

    def columns_of(block, half, start, size):
        return weight[pl.ds(pl.multiple_of(block * 1280 + half * WIDTH + start, 16), size)]

    for k in range(8):
        twin_arrived(k)
    for head in range(HEADS):
        for d in range(2):
            half = gathered.at[
                lax.rem(x + 2, 4), pl.ds(d * (TOK // 2), TOK // 2), lanes(head)
            ]
            arrived(half, f_send.at[d, head], f_recv.at[d, head])
    halves = (1 - h, h)
    for step, shift in enumerate((0, 1, 3)):
        block = lax.rem(zh + shift, 4)
        for i, half in enumerate(halves):
            term = dot_nt(gathered[block], columns_of(block, half, 0, WIDTH))
            acc[i] = term if step == 0 else acc[i] + term
    pump(8)
    twin_arrived(8)
    block = lax.rem(zh + 2, 4)
    for i, half in enumerate(halves):
        for c, (start, size) in enumerate(COLUMNS):
            where = slice(start, start + size)
            term = acc[i, :, where] + dot_nt(
                gathered[block], columns_of(block, half, start, size)
            )
            if i == 1:
                term = latent_ref[:, where].astype(jnp.float32) + gate_ref[0:1, where] * term
            staged[i, :, where] = term.astype(jnp.bfloat16)
            send(
                staged.at[i, :, where],
                landed.at[i, :, where],
                o_send.at[i, c],
                o_recv.at[i, c],
                following,
                ten if i else other,
            )

    arrived(gate_prev, gate_send, gate_recv)
    for c, (start, size) in enumerate(COLUMNS):
        where = slice(start, start + size)
        for i in range(2):
            arrived(landed.at[i, :, where], o_send.at[i, c], o_recv.at[i, c])
        out_ref[:, where] = (
            landed[1, :, where].astype(jnp.float32)
            + gate_prev[0:1, where] * landed[0, :, where].astype(jnp.float32)
        ).astype(jnp.bfloat16)

    for copy in sent:
        copy.wait_send()


def body(
    queries,
    keys,
    values,
    q_gain,
    k_gain,
    frame_offset,
    noise_level,
    gate_table,
    out_weight,
    latent,
    fresh,
):
    half_width = HD // 2
    pair_rate = jnp.exp(
        jnp.arange(half_width, dtype=jnp.float32) * (-math.log(10000.0) / half_width)
    )
    angles = frame_offset[0].astype(jnp.float32) * pair_rate
    cosines, sines = jnp.cos(angles), jnp.sin(angles)
    straight = jnp.concatenate([cosines, cosines])
    crossed = jnp.concatenate([-sines, sines])

    def tables(gain, factor):
        by_head = gain.reshape(HEADS, HD) * factor
        swapped = jnp.concatenate([by_head[:, half_width:], by_head[:, :half_width]], axis=1)
        return [(by_head * straight).reshape(-1), (swapped * crossed).reshape(-1)]

    table = jnp.stack(
        tables(q_gain, math.log2(math.e) / math.sqrt(HD)) + tables(k_gain, 1.0)
        + [jnp.zeros((WIDTH,), jnp.float32)] * 4
    )
    gate_row = lax.dynamic_index_in_dim(gate_table, noise_level[0], 0, keepdims=True)
    gate = jnp.broadcast_to(gate_row, (8, WIDTH))

    bf16, f32 = jnp.bfloat16, jnp.float32
    dma = pltpu.SemaphoreType.DMA
    moved = pl.pallas_call(
        kernel,
        out_shape=jax.ShapeDtypeStruct((TOK, WIDTH), bf16),
        in_specs=[pl.BlockSpec(memory_space=pltpu.VMEM)] * 7,
        out_specs=pl.BlockSpec(memory_space=pltpu.VMEM),
        scratch_shapes=[
            pltpu.VMEM((8, 8, TOK), f32),
            pltpu.VMEM((TOK, WIDTH), bf16),
            pltpu.VMEM((3 * TOK, WIDTH), bf16),
            pltpu.VMEM((2 * TOK, WIDTH), bf16),
            pltpu.VMEM((HEADS, TOK, HD), f32),
            pltpu.VMEM((HEADS, TOK, HD), f32),
            pltpu.VMEM((HEADS, TOK, HD), f32),
            pltpu.VMEM((4, TOK, WIDTH), bf16),
            pltpu.VMEM((D, WIDTH), bf16),
            pltpu.VMEM((2, TOK, WIDTH), f32),
            pltpu.VMEM((2, TOK, WIDTH), bf16),
            pltpu.VMEM((2, TOK, WIDTH), bf16),
            pltpu.VMEM((8, WIDTH), f32),
            dma((7,)),
            dma((7,)),
            dma((4,)),
            dma((4,)),
            dma,
            dma,
            dma,
            dma,
            dma,
            dma,
            dma((2, 15)),
            dma((2, 15)),
            dma((32,)),
            dma((32,)),
            dma((2, HEADS)),
            dma((2, HEADS)),
            dma((2, HEADS)),
            dma((2, HEADS)),
            dma((2, len(COLUMNS))),
            dma((2, len(COLUMNS))),
        ],
        compiler_params=pltpu.CompilerParams(
            collective_id=0, has_side_effects=True, vmem_limit_bytes=48 * 1024 * 1024
        ),
        cost_estimate=pl.CostEstimate(
            flops=3_700_000_000, bytes_accessed=4_000_000, transcendentals=2_300_000
        ),
    )(queries, keys, values, table, gate, latent, out_weight.T)
    return jnp.where(lax.axis_index("section") == 0, fresh, moved)


def solution(mesh):
    in_specs = (
        P("section", "tensor"),
        P("section", "tensor"),
        P("section", "tensor"),
        P("tensor"),
        P("tensor"),
        P("section"),
        P("section"),
        P(None, "tensor"),
        P("tensor", "section"),
        P("section", "tensor"),
        P(None, "tensor"),
    )
    out_specs = P("section", "tensor")
    return jax.shard_map(body, mesh=mesh, in_specs=in_specs, out_specs=out_specs, check_vma=False)
```

```python
import math

import jax
import jax.numpy as jnp
from jax import lax
from jax.experimental import pallas as pl
from jax.experimental.pallas import tpu as pltpu
from jax.sharding import PartitionSpec as P

D = 5120
HD = 128
EPSILON = 1e-06
TOK = 384
WIDTH = 640
HEADS = WIDTH // HD
SLAB = 80
MASKED = -1e30
PIECES = ((0, 2), (2, 1), (3, 2))
NT = (((1,), (1,)), ((), ()))


def dot_nt(a, b):
    return lax.dot_general(a, b, NT, preferred_element_type=jnp.float32)


def dot_nn(a, b):
    return jnp.dot(a, b, preferred_element_type=jnp.float32)


def kernel(
    offset_ref,
    level_ref,
    gain_ref,
    q_hbm,
    k_hbm,
    v_hbm,
    gate_hbm,
    latent_hbm,
    slab_ref,
    out_ref,
    q_ref,
    k_ref,
    v_ref,
    gate_table,
    latent_ref,
    gate_ref,
    load_sem,
    squares,
    q_n,
    k_all,
    v_all,
    peak,
    total,
    mixed,
    gathered,
    weight,
    staged,
    landed,
    gate_prev,
    sq_send,
    sq_recv,
    halo_send,
    halo_recv,
    gate_send,
    gate_recv,
    swap_send,
    swap_recv,
    side_send,
    side_recv,
    ring_send,
    ring_recv,
    twin_send,
    twin_recv,
    a_send,
    a_recv,
    f_send,
    f_recv,
    o_send,
    o_recv,
):
    sec = lax.axis_index("section")
    ten = lax.axis_index("tensor")
    z = lax.div(sec, 4)
    zh = lax.div(sec, 16)
    core = lax.rem(sec, 2)
    yl = lax.rem(lax.div(sec, 2), 2)
    x = lax.div(ten, 2)
    h = lax.rem(ten, 2)
    near = sec + 1 - 2 * core
    far = lax.rem(sec + 2 * core + 63, 64)
    following = lax.rem(sec + 1, 64)
    previous = lax.rem(sec + 63, 64)
    z_next = lax.rem(sec + 4, 64)
    z_last = lax.rem(sec + 60, 64)
    y_side = sec + 2 - 4 * yl
    x_right = lax.rem(x + 1, 4) * 2 + h
    x_left = lax.rem(x + 3, 4) * 2 + h
    other = ten + 1 - 2 * h
    swap_sec = 16 * x + lax.rem(sec, 16)
    swap_ten = 2 * zh + h
    stays = x == zh

    def remote(src, dst, send, recv, section, tensor):
        return pltpu.make_async_remote_copy(
            src_ref=src,
            dst_ref=dst,
            send_sem=send,
            recv_sem=recv,
            device_id={"section": section, "tensor": tensor},
            device_id_type=pl.DeviceIdType.MESH,
        )

    loads = [
        pltpu.make_async_copy(src, dst, load_sem.at[i])
        for i, (src, dst) in enumerate(
            (
                (k_hbm, k_ref),
                (q_hbm, q_ref),
                (v_hbm, v_ref),
                (gate_hbm, gate_table),
            )
            + tuple(
                (latent_hbm.at[:, pl.ds(t * HD, HD)], latent_ref.at[t]) for t in range(HEADS)
            )
        )
    ]
    for load in loads:
        load.start()

    sent = []

    def send(src, dst, send_sem, recv_sem, section, tensor):
        copy = remote(src, dst, send_sem, recv_sem, section, tensor)
        copy.start()
        sent.append(copy)

    def arrived(dst, send_sem, recv_sem):
        remote(dst, dst, send_sem, recv_sem, near, ten).wait_recv()

    barrier = pltpu.get_barrier_semaphore()
    greeted = [(near, ten), (far, ten), (z_next, ten), (z_last, ten), (y_side, ten)]
    greeted += [(following, ten), (following, other), (previous, ten), (previous, other)]
    greeted += [(sec, lax.rem(ten + i, 8)) for i in range(1, 8)]
    for section, tensor in greeted:
        pl.semaphore_signal(
            barrier,
            inc=1,
            device_id={"section": section, "tensor": tensor},
            device_id_type=pl.DeviceIdType.MESH,
        )

    @pl.when(jnp.logical_not(stays))
    def _():
        pl.semaphore_signal(
            barrier,
            inc=1,
            device_id={"section": swap_sec, "tensor": swap_ten},
            device_id_type=pl.DeviceIdType.MESH,
        )

    def lanes(head):
        return slice(head * HD, (head + 1) * HD)

    def row_sums(ref):
        part = jnp.zeros((TOK, HD), jnp.float32)
        for head in range(HEADS):
            wide = ref[:, lanes(head)].astype(jnp.float32)
            part += wide * wide
        return jnp.sum(part.T, axis=0, keepdims=True)

    lane = lax.broadcasted_iota(jnp.int32, (1, HD), 1)
    pair = lax.rem(lane, HD // 2).astype(jnp.float32)
    angles = offset_ref[0].astype(jnp.float32) * jnp.exp(
        pair * (-math.log(10000.0) / (HD // 2))
    )
    straight = jnp.cos(angles)
    crossed = jnp.where(lane < HD // 2, -1.0, 1.0) * jnp.sin(angles)

    loads[0].wait()
    k_sums = row_sums(k_ref)
    loads[1].wait()
    q_sums = row_sums(q_ref)
    row = lax.broadcasted_iota(jnp.int32, (8, TOK), 0)
    squares[ten] = jnp.where(row < 4, q_sums, k_sums)

    pl.semaphore_wait(barrier, len(greeted) + jnp.where(stays, 0, 1))

    for i in range(1, 8):
        send(
            squares.at[ten], squares.at[ten], sq_send.at[i - 1], sq_recv.at[i - 1], sec,
            lax.rem(ten + i, 8),
        )

    def slab(zz, j, c):
        place = 4 * lax.rem(zz + 16, 16) + 2 * ((1 - yl) if j else yl) + c
        return weight.at[pl.ds(pl.multiple_of(place * SLAB, 16), SLAB)]

    swap = remote(
        slab_ref,
        weight.at[pl.ds(pl.multiple_of(swap_sec * SLAB, 16), SLAB)],
        swap_send,
        swap_recv,
        swap_sec,
        swap_ten,
    )
    keep = pltpu.make_async_copy(slab_ref, slab(z, 0, core), swap_send)

    @pl.when(jnp.logical_not(stays))
    def _():
        swap.start()

    @pl.when(stays)
    def _():
        keep.start()

    mine, by_near, by_far = (pl.ds(i * TOK, TOK) for i in range(3))
    v_near, v_far = v_all.at[pl.ds(0, TOK)], v_all.at[pl.ds(TOK, TOK)]
    send(v_hbm, v_far, halo_send.at[0], halo_recv.at[0], far, ten)
    send(v_hbm, v_near, halo_send.at[1], halo_recv.at[1], near, ten)

    def number(k, j):
        return 14 if k == 8 else 2 * (k - 1) + j

    def origin(d, k):
        return z + k if d else z - k

    def ring(d, k, j):
        n = number(k, j)
        piece = slab(origin(d, k - 1), j, core)
        return remote(
            piece, piece, ring_send.at[d, n], ring_recv.at[d, n], z_last if d else z_next, ten
        )

    def across(d, k):
        piece = slab(origin(d, k), 0, core)
        d, n = (1 if k == 8 else d), number(k, 1)
        return remote(piece, piece, ring_send.at[d, n], ring_recv.at[d, n], y_side, ten)

    def twin_copy(piece, m):
        return remote(piece, piece, twin_send.at[m], twin_recv.at[m], near, ten)

    def directions(k, j):
        return (j,) if k == 8 else (0, 1)

    even, odd = core == 0, core == 1

    def first(j):
        for d in range(2):
            if j == 0:
                ring(d, 1, 0).start()
            else:

                @pl.when(odd)
                def _(d=d):
                    ring(d, 1, 1).start()

        twin_copy(slab(z, j, core), j).start()

    def second_column(k, forward):
        for d in directions(k, 1):
            n = number(k, 1)
            piece = slab(origin(d, k), 1, core)
            arrived(piece, ring_send.at[d, n], ring_recv.at[d, n])
            if forward and (k < 7 or (k == 7 and d == 1)):
                ring(d, k + 1, 1).start()
            twin_copy(piece, 2 + 15 * d + n).start()

    def pump(k):
        for d in directions(k, 0):
            n = number(k, 0)
            piece = slab(origin(d, k), 0, core)
            arrived(piece, ring_send.at[d, n], ring_recv.at[d, n])
            if k < 7 or (k == 7 and d == 0):
                ring(d, k + 1, 0).start()

            @pl.when(even)
            def _(d=d):
                across(d, k).start()

            twin_copy(piece, 2 + 15 * d + n).start()

        @pl.when(odd)
        def _():
            second_column(k, True)

        if 1 < k < 8:
            second_of_even(k - 1)

    def second_of_even(k):
        @pl.when(even)
        def _():
            second_column(k, False)

    def ring_sent():
        for m in range(2):
            twin_copy(slab(z, m, core), m).wait_send()
        for k in range(1, 9):
            for j in range(2):
                for d in directions(k, j):
                    n = number(k, j)
                    remote(
                        slab(z, 0, core), slab(z, 0, core), ring_send.at[d, n],
                        ring_recv.at[d, n], near, ten,
                    ).wait_send()
                    twin_copy(slab(origin(d, k), j, core), 2 + 15 * d + n).wait_send()

    def twin_arrived(k):
        if k == 0:
            for j in range(2):
                arrived(slab(z, j, 1 - core), twin_send.at[j], twin_recv.at[j])
            return
        for j in range(2):
            for d in range(2):
                if k == 8 and j != d:
                    continue
                m = 2 + 15 * d + number(k, j)
                arrived(slab(origin(d, k), j, 1 - core), twin_send.at[m], twin_recv.at[m])

    for i in range(1, 8):
        arrived(squares.at[lax.rem(ten + 8 - i, 8)], sq_send.at[i - 1], sq_recv.at[i - 1])
    sums = squares[0]
    for i in range(1, 8):
        sums = sums + squares[i]
    scale = lax.rsqrt(sums / D + EPSILON)
    q_scale = jnp.broadcast_to(scale[0:1] * (math.log2(math.e) / math.sqrt(HD)), (HD, TOK)).T
    k_scale = jnp.broadcast_to(scale[4:5], (HD, TOK)).T

    def rotated(ref, head, at, by):
        wide = ref[:, lanes(head)].astype(jnp.float32)
        gain = gain_ref[at : at + 1, lanes(head)]
        turned = wide * (gain * straight) + pltpu.roll(wide, HD // 2, 1) * (
            pltpu.roll(gain, HD // 2, 1) * crossed
        )
        return (turned * by).astype(jnp.bfloat16)

    for head in range(HEADS):
        k_all[mine, lanes(head)] = rotated(k_ref, head, 1, k_scale)
    send(k_all.at[mine], k_all.at[by_far], halo_send.at[2], halo_recv.at[2], far, ten)
    send(k_all.at[mine], k_all.at[by_near], halo_send.at[3], halo_recv.at[3], near, ten)
    for head in range(HEADS):
        q_n[:, lanes(head)] = rotated(q_ref, head, 0, q_scale)

    loads[2].wait()
    arrived(v_near, halo_send.at[1], halo_recv.at[1])
    arrived(k_all.at[by_near], halo_send.at[3], halo_recv.at[3])
    for head in range(HEADS):
        scores = dot_nt(q_n[:, lanes(head)], k_all[0 : 2 * TOK, lanes(head)])
        highest = jnp.max(scores, axis=-1, keepdims=True)
        raised = jnp.exp2(scores - highest)
        peak[head] = jnp.broadcast_to(highest, (TOK, HD))
        total[head] = jnp.broadcast_to(jnp.sum(raised, axis=-1, keepdims=True), (TOK, HD))
        raised = raised.astype(jnp.bfloat16)
        mixed[head] = dot_nn(raised[:, :TOK], v_ref[:, lanes(head)]) + dot_nn(
            raised[:, TOK:], v_all[0:TOK, lanes(head)]
        )

    @pl.when(jnp.logical_not(stays))
    def _():
        swap.wait_send()
        arrived(slab(z, 0, core), swap_send, swap_recv)

    @pl.when(stays)
    def _():
        keep.wait()

    own_slab = slab(z, 0, core)
    first(0)
    send(own_slab, own_slab, side_send, side_recv, y_side, ten)

    loads[3].wait()
    gate_row = gate_table[pl.ds(level_ref[0], 1), :]
    for t in range(HEADS):
        gate_ref[t] = jnp.broadcast_to(gate_row[:, lanes(t)], (8, HD))
    send(gate_ref, gate_prev, gate_send, gate_recv, following, ten)
    for load in loads[4:]:
        load.wait()
    arrived(slab(z, 1, core), side_send, side_recv)
    first(1)
    pump(1)
    pump(2)
    pump(3)
    pump(4)

    arrived(v_far, halo_send.at[0], halo_recv.at[0])
    arrived(k_all.at[by_far], halo_send.at[2], halo_recv.at[2])
    absent = jnp.where((sec == 0) | (sec == 63), MASKED, 0.0)

    def pass_on(head):
        for d in range(2):
            source = lax.rem(x + (1 if d else 3), 4)
            here = gathered.at[source, :, lanes(head)]
            arrived(here, a_send.at[d, head], a_recv.at[d, head])
            half = gathered.at[source, pl.ds(d * (TOK // 2), TOK // 2), lanes(head)]
            send(half, half, f_send.at[d, head], f_recv.at[d, head], sec, x_left if d else x_right)

    for head in range(HEADS):
        scores = dot_nt(q_n[:, lanes(head)], k_all[2 * TOK :, lanes(head)]) + absent
        before = peak[head]
        highest = jnp.maximum(before[:, 0:1], jnp.max(scores, axis=-1, keepdims=True))
        raised = jnp.exp2(scores - highest)
        shrink = jnp.exp2(before - highest)
        sums = total[head] * shrink + jnp.sum(raised, axis=-1, keepdims=True)
        result = mixed[head] * shrink + dot_nn(
            raised.astype(jnp.bfloat16), v_all[TOK : 2 * TOK, lanes(head)]
        )
        gathered[x, :, lanes(head)] = (result / sums).astype(jnp.bfloat16)
        own = gathered.at[x, :, lanes(head)]
        for d in range(2):
            send(own, own, a_send.at[d, head], a_recv.at[d, head], sec, x_left if d else x_right)
        if head == 2:
            pump(5)
            pass_on(0)
    pass_on(1)
    pass_on(2)
    pump(6)
    pass_on(3)
    pass_on(4)
    pump(7)

    def project(half, piece, first_tile, tiles):
        own = half == h
        i = jnp.where(own, 1, 0)
        value = jnp.zeros((TOK, tiles * HD), jnp.float32)
        for block in range(4):
            start = block * 1280 + half * WIDTH + first_tile * HD
            value += dot_nt(
                gathered[block], weight[pl.ds(pl.multiple_of(start, HD), tiles * HD), :]
            )
        for t in range(tiles):
            part = value[:, lanes(t)]
            updated = (
                latent_ref[first_tile + t].astype(jnp.float32) + gate_ref[first_tile + t][0:1] * part
            )
            staged[i, first_tile + t] = jnp.where(own, updated, part).astype(jnp.bfloat16)
        send(
            staged.at[i, pl.ds(first_tile, tiles)],
            landed.at[i, pl.ds(first_tile, tiles)],
            o_send.at[i, piece],
            o_recv.at[i, piece],
            following,
            jnp.where(own, ten, other),
        )

    def project_side(shift):
        column = lax.rem(z + shift, 4)
        side = lax.rem(column, 2)
        project(lax.div(column, 2), 2 * side, 3 * side, 2)

    def project_middle(shift):
        project(lax.div(lax.rem(z + shift, 4), 2), 1, 2, 1)

    for k in range(7):
        twin_arrived(k)
    for head in range(HEADS):
        for d in range(2):
            half = gathered.at[lax.rem(x + 2, 4), pl.ds(d * (TOK // 2), TOK // 2), lanes(head)]
            arrived(half, f_send.at[d, head], f_recv.at[d, head])
    project_side(2)
    second_of_even(7)
    twin_arrived(7)
    project_side(1)
    pump(8)
    project_side(3)
    project_middle(2)
    second_of_even(8)
    twin_arrived(8)
    project_side(0)
    project_middle(0)

    ring_sent()
    for copy in sent:
        copy.wait_send()
    arrived(gate_prev, gate_send, gate_recv)
    for c, (start, size) in enumerate(PIECES):
        for i in range(2):
            arrived(landed.at[i, pl.ds(start, size)], o_send.at[i, c], o_recv.at[i, c])
        for t in range(start, start + size):
            out_ref[:, lanes(t)] = (
                landed[1, t].astype(jnp.float32)
                + gate_prev[t][0:1] * landed[0, t].astype(jnp.float32)
            ).astype(jnp.bfloat16)


def body(
    queries,
    keys,
    values,
    q_gain,
    k_gain,
    frame_offset,
    noise_level,
    gate_table,
    out_weight,
    latent,
    fresh,
):
    gains = jnp.stack([q_gain, k_gain])
    bf16, f32 = jnp.bfloat16, jnp.float32
    dma = pltpu.SemaphoreType.DMA
    moved = pl.pallas_call(
        kernel,
        out_shape=jax.ShapeDtypeStruct((TOK, WIDTH), bf16),
        in_specs=[pl.BlockSpec(memory_space=pltpu.SMEM)] * 2
        + [pl.BlockSpec(memory_space=pltpu.VMEM)]
        + [pl.BlockSpec(memory_space=pltpu.HBM)] * 6,
        out_specs=pl.BlockSpec(memory_space=pltpu.VMEM),
        scratch_shapes=[
            pltpu.VMEM((TOK, WIDTH), bf16),
            pltpu.VMEM((TOK, WIDTH), bf16),
            pltpu.VMEM((TOK, WIDTH), bf16),
            pltpu.VMEM((128, WIDTH), f32),
            pltpu.VMEM((HEADS, TOK, HD), bf16),
            pltpu.VMEM((HEADS, 8, HD), f32),
            dma((4 + HEADS,)),
            pltpu.VMEM((8, 8, TOK), f32),
            pltpu.VMEM((TOK, WIDTH), bf16),
            pltpu.VMEM((3 * TOK, WIDTH), bf16),
            pltpu.VMEM((2 * TOK, WIDTH), bf16),
            pltpu.VMEM((HEADS, TOK, HD), f32),
            pltpu.VMEM((HEADS, TOK, HD), f32),
            pltpu.VMEM((HEADS, TOK, HD), f32),
            pltpu.VMEM((4, TOK, WIDTH), bf16),
            pltpu.VMEM((D, WIDTH), bf16),
            pltpu.VMEM((2, HEADS, TOK, HD), bf16),
            pltpu.VMEM((2, HEADS, TOK, HD), bf16),
            pltpu.VMEM((HEADS, 8, HD), f32),
            dma((7,)),
            dma((7,)),
            dma((4,)),
            dma((4,)),
            dma,
            dma,
            dma,
            dma,
            dma,
            dma,
            dma((2, 15)),
            dma((2, 15)),
            dma((32,)),
            dma((32,)),
            dma((2, HEADS)),
            dma((2, HEADS)),
            dma((2, HEADS)),
            dma((2, HEADS)),
            dma((2, len(PIECES))),
            dma((2, len(PIECES))),
        ],
        compiler_params=pltpu.CompilerParams(
            collective_id=0, has_side_effects=True, vmem_limit_bytes=60 * 1024 * 1024
        ),
        cost_estimate=pl.CostEstimate(
            flops=3_700_000_000, bytes_accessed=4_000_000, transcendentals=2_300_000
        ),
    )(
        frame_offset, noise_level, gains, queries, keys, values, gate_table, latent, out_weight.T
    )
    return jnp.where(lax.axis_index("section") == 0, fresh, moved)


def solution(mesh):
    in_specs = (
        P("section", "tensor"),
        P("section", "tensor"),
        P("section", "tensor"),
        P("tensor"),
        P("tensor"),
        P("section"),
        P("section"),
        P(None, "tensor"),
        P("tensor", "section"),
        P("section", "tensor"),
        P(None, "tensor"),
    )
    out_specs = P("section", "tensor")
    return jax.shard_map(body, mesh=mesh, in_specs=in_specs, out_specs=out_specs, check_vma=False)
```

```python
import math

import jax
import jax.numpy as jnp
from jax import lax
from jax.experimental import pallas as pl
from jax.experimental.pallas import tpu as pltpu
from jax.sharding import PartitionSpec as P

D = 5120
HD = 128
EPSILON = 1e-06
TOK = 384
WIDTH = 640
HEADS = WIDTH // HD
SLAB = 80
MASKED = -1e30
PARTS = ((0, 48), (48, 32))
LAG = 3
PIECES = ((0, 2), (2, 1), (3, 2))
NT = (((1,), (1,)), ((), ()))


def dot_nt(a, b):
    return lax.dot_general(a, b, NT, preferred_element_type=jnp.float32)


def dot_nn(a, b):
    return jnp.dot(a, b, preferred_element_type=jnp.float32)


def kernel(
    offset_ref,
    level_ref,
    gain_ref,
    q_hbm,
    k_hbm,
    v_hbm,
    gate_hbm,
    latent_hbm,
    slab_ref,
    out_ref,
    q_ref,
    k_ref,
    v_ref,
    gate_table,
    latent_ref,
    gate_ref,
    load_sem,
    squares,
    q_n,
    k_all,
    v_all,
    peak,
    total,
    mixed,
    gathered,
    weight,
    staged,
    landed,
    gate_prev,
    sq_send,
    sq_recv,
    halo_send,
    halo_recv,
    gate_send,
    gate_recv,
    swap_send,
    swap_recv,
    side_send,
    side_recv,
    ring_send,
    ring_recv,
    twin_send,
    twin_recv,
    a_send,
    a_recv,
    f_send,
    f_recv,
    o_send,
    o_recv,
):
    sec = lax.axis_index("section")
    ten = lax.axis_index("tensor")
    z = lax.div(sec, 4)
    zh = lax.div(sec, 16)
    core = lax.rem(sec, 2)
    yl = lax.rem(lax.div(sec, 2), 2)
    x = lax.div(ten, 2)
    h = lax.rem(ten, 2)
    near = sec + 1 - 2 * core
    far = lax.rem(sec + 2 * core + 63, 64)
    following = lax.rem(sec + 1, 64)
    previous = lax.rem(sec + 63, 64)
    z_next = lax.rem(sec + 4, 64)
    z_last = lax.rem(sec + 60, 64)
    y_side = sec + 2 - 4 * yl
    x_right = lax.rem(x + 1, 4) * 2 + h
    x_left = lax.rem(x + 3, 4) * 2 + h
    other = ten + 1 - 2 * h
    swap_sec = 16 * x + lax.rem(sec, 16)
    swap_ten = 2 * zh + h
    stays = x == zh

    def remote(src, dst, send, recv, section, tensor):
        return pltpu.make_async_remote_copy(
            src_ref=src,
            dst_ref=dst,
            send_sem=send,
            recv_sem=recv,
            device_id={"section": section, "tensor": tensor},
            device_id_type=pl.DeviceIdType.MESH,
        )

    loads = [
        pltpu.make_async_copy(src, dst, load_sem.at[i])
        for i, (src, dst) in enumerate(
            (
                (k_hbm, k_ref),
                (q_hbm, q_ref),
                (v_hbm, v_ref),
                (gate_hbm, gate_table),
            )
            + tuple(
                (latent_hbm.at[:, pl.ds(t * HD, HD)], latent_ref.at[t]) for t in range(HEADS)
            )
        )
    ]
    for load in loads:
        load.start()

    sent = []

    def send(src, dst, send_sem, recv_sem, section, tensor):
        copy = remote(src, dst, send_sem, recv_sem, section, tensor)
        copy.start()
        sent.append(copy)

    def arrived(dst, send_sem, recv_sem):
        remote(dst, dst, send_sem, recv_sem, near, ten).wait_recv()

    barrier = pltpu.get_barrier_semaphore()
    greeted = [(near, ten), (far, ten), (z_next, ten), (z_last, ten), (y_side, ten)]
    greeted += [(following, ten), (following, other), (previous, ten), (previous, other)]
    greeted += [(sec, lax.rem(ten + i, 8)) for i in range(1, 8)]
    for section, tensor in greeted:
        pl.semaphore_signal(
            barrier,
            inc=1,
            device_id={"section": section, "tensor": tensor},
            device_id_type=pl.DeviceIdType.MESH,
        )

    @pl.when(jnp.logical_not(stays))
    def _():
        pl.semaphore_signal(
            barrier,
            inc=1,
            device_id={"section": swap_sec, "tensor": swap_ten},
            device_id_type=pl.DeviceIdType.MESH,
        )

    def lanes(head):
        return slice(head * HD, (head + 1) * HD)

    def row_sums(ref):
        part = jnp.zeros((TOK, HD), jnp.float32)
        for head in range(HEADS):
            wide = ref[:, lanes(head)].astype(jnp.float32)
            part += wide * wide
        return jnp.sum(part.T, axis=0, keepdims=True)

    lane = lax.broadcasted_iota(jnp.int32, (1, HD), 1)
    pair = lax.rem(lane, HD // 2).astype(jnp.float32)
    angles = offset_ref[0].astype(jnp.float32) * jnp.exp(
        pair * (-math.log(10000.0) / (HD // 2))
    )
    straight = jnp.cos(angles)
    crossed = jnp.where(lane < HD // 2, -1.0, 1.0) * jnp.sin(angles)

    loads[0].wait()
    k_sums = row_sums(k_ref)
    loads[1].wait()
    q_sums = row_sums(q_ref)
    row = lax.broadcasted_iota(jnp.int32, (8, TOK), 0)
    squares[ten] = jnp.where(row < 4, q_sums, k_sums)

    pl.semaphore_wait(barrier, len(greeted) + jnp.where(stays, 0, 1))

    for i in range(1, 8):
        send(
            squares.at[ten], squares.at[ten], sq_send.at[i - 1], sq_recv.at[i - 1], sec,
            lax.rem(ten + i, 8),
        )

    def slab(zz, j, c):
        place = 4 * lax.rem(zz + 16, 16) + 2 * ((1 - yl) if j else yl) + c
        return weight.at[pl.ds(pl.multiple_of(place * SLAB, 16), SLAB)]

    swap = remote(
        slab_ref,
        weight.at[pl.ds(pl.multiple_of(swap_sec * SLAB, 16), SLAB)],
        swap_send,
        swap_recv,
        swap_sec,
        swap_ten,
    )
    keep = pltpu.make_async_copy(slab_ref, slab(z, 0, core), swap_send)

    @pl.when(jnp.logical_not(stays))
    def _():
        swap.start()

    @pl.when(stays)
    def _():
        keep.start()

    mine, by_near, by_far = (pl.ds(i * TOK, TOK) for i in range(3))
    v_near, v_far = v_all.at[pl.ds(0, TOK)], v_all.at[pl.ds(TOK, TOK)]
    for head in range(HEADS):
        send(
            v_hbm.at[:, lanes(head)], v_far.at[:, lanes(head)], halo_send.at[9 + head],
            halo_recv.at[9 + head], far, ten,
        )
    send(v_hbm, v_near, halo_send.at[1], halo_recv.at[1], near, ten)

    def number(k, j):
        return 14 if k == 8 else 2 * (k - 1) + j

    def origin(d, k):
        return z + k if d else z - k

    def part_of(zz, j, p):
        start, size = PARTS[p]
        place = 4 * lax.rem(zz + 16, 16) + 2 * ((1 - yl) if j else yl) + core
        return weight.at[pl.ds(pl.multiple_of(place * SLAB + start, 16), size)]

    def ring(d, k, j, p):
        n = number(k, j)
        piece = part_of(origin(d, k - 1), j, p)
        return remote(
            piece, piece, ring_send.at[d, n, p], ring_recv.at[d, n, p], z_last if d else z_next, ten
        )

    def across(d, k):
        piece = slab(origin(d, k), 0, core)
        d, n = (1 if k == 8 else d), number(k, 1)
        return remote(piece, piece, ring_send.at[d, n, 0], ring_recv.at[d, n, 0], y_side, ten)

    def twin_copy(piece, m):
        return remote(piece, piece, twin_send.at[m], twin_recv.at[m], near, ten)

    def directions(k, j):
        return (j,) if k == 8 else (0, 1)

    even, odd = core == 0, core == 1

    parts = range(len(PARTS))

    def first(j):
        def start():
            for p in parts:
                for d in range(2):
                    ring(d, 1, j, p).start()

        if j == 0:
            start()
        else:
            pl.when(odd)(start)
        twin_copy(slab(z, j, core), j).start()

    def pass_slab(k, j):
        n = number(k, j)
        for p in parts:
            for d in directions(k, j):
                arrived(part_of(origin(d, k), j, p), ring_send.at[d, n, p], ring_recv.at[d, n, p])
                if k < 7 or (k == 7 and d == j):
                    ring(d, k + 1, j, p).start()
                if p == len(PARTS) - 1:
                    if j == 0:

                        @pl.when(even)
                        def _(d=d):
                            across(d, k).start()

                    twin_copy(slab(origin(d, k), j, core), 2 + 15 * d + n).start()

    def pump(k):
        pass_slab(k, 0)

        @pl.when(odd)
        def _():
            pass_slab(k, 1)

        if LAG < k < 8:
            second_of_even(k - LAG)

    def second_of_even(k):
        @pl.when(even)
        def _():
            n = number(k, 1)
            for d in directions(k, 1):
                piece = slab(origin(d, k), 1, core)
                arrived(piece, ring_send.at[d, n, 0], ring_recv.at[d, n, 0])
                twin_copy(piece, 2 + 15 * d + n).start()

    def ring_sent():
        for m in range(2):
            twin_copy(slab(z, m, core), m).wait_send()
        for k in range(1, 9):
            for j in range(2):
                for d in directions(k, j):
                    twin_copy(slab(origin(d, k), j, core), 2 + 15 * d + number(k, j)).wait_send()
                    if j == 0:
                        for p in parts:
                            ring(d, k, 0, p).wait_send()

        @pl.when(odd)
        def _():
            for k in range(1, 9):
                for d in directions(k, 1):
                    for p in parts:
                        ring(d, k, 1, p).wait_send()

        @pl.when(even)
        def _():
            for k in range(1, 9):
                for d in directions(k, 0):
                    across(d, k).wait_send()

    def twin_arrived(k):
        if k == 0:
            for j in range(2):
                arrived(slab(z, j, 1 - core), twin_send.at[j], twin_recv.at[j])
            return
        for j in range(2):
            for d in range(2):
                if k == 8 and j != d:
                    continue
                m = 2 + 15 * d + number(k, j)
                arrived(slab(origin(d, k), j, 1 - core), twin_send.at[m], twin_recv.at[m])

    for i in range(1, 8):
        arrived(squares.at[lax.rem(ten + 8 - i, 8)], sq_send.at[i - 1], sq_recv.at[i - 1])
    sums = squares[0]
    for i in range(1, 8):
        sums = sums + squares[i]
    scale = lax.rsqrt(sums / D + EPSILON)
    q_scale = jnp.broadcast_to(scale[0:1] * (math.log2(math.e) / math.sqrt(HD)), (HD, TOK)).T
    k_scale = jnp.broadcast_to(scale[4:5], (HD, TOK)).T

    def rotated(ref, head, at, by):
        wide = ref[:, lanes(head)].astype(jnp.float32)
        gain = gain_ref[at : at + 1, lanes(head)]
        turned = wide * (gain * straight) + pltpu.roll(wide, HD // 2, 1) * (
            pltpu.roll(gain, HD // 2, 1) * crossed
        )
        return (turned * by).astype(jnp.bfloat16)

    for head in range(HEADS):
        k_all[mine, lanes(head)] = rotated(k_ref, head, 1, k_scale)
        send(
            k_all.at[mine, lanes(head)], k_all.at[by_far, lanes(head)], halo_send.at[4 + head],
            halo_recv.at[4 + head], far, ten,
        )
    send(k_all.at[mine], k_all.at[by_near], halo_send.at[3], halo_recv.at[3], near, ten)
    for head in range(HEADS):
        q_n[:, lanes(head)] = rotated(q_ref, head, 0, q_scale)

    @pl.when(jnp.logical_not(stays))
    def _():
        swap.wait_send()
        arrived(slab(z, 0, core), swap_send, swap_recv)

    @pl.when(stays)
    def _():
        keep.wait()

    own_slab = slab(z, 0, core)
    first(0)
    send(own_slab, own_slab, side_send, side_recv, y_side, ten)

    loads[3].wait()
    gate_row = gate_table[pl.ds(level_ref[0], 1), :]
    for t in range(HEADS):
        gate_ref[t] = jnp.broadcast_to(gate_row[:, lanes(t)], (8, HD))
    send(gate_ref, gate_prev, gate_send, gate_recv, following, ten)
    for load in loads[4:]:
        load.wait()
    arrived(slab(z, 1, core), side_send, side_recv)
    first(1)

    loads[2].wait()
    arrived(v_near, halo_send.at[1], halo_recv.at[1])
    arrived(k_all.at[by_near], halo_send.at[3], halo_recv.at[3])
    for head in range(HEADS):
        scores = dot_nt(q_n[:, lanes(head)], k_all[0 : 2 * TOK, lanes(head)])
        highest = jnp.max(scores, axis=-1, keepdims=True)
        raised = jnp.exp2(scores - highest)
        peak[head] = jnp.broadcast_to(highest, (TOK, HD))
        total[head] = jnp.broadcast_to(jnp.sum(raised, axis=-1, keepdims=True), (TOK, HD))
        raised = raised.astype(jnp.bfloat16)
        mixed[head] = dot_nn(raised[:, :TOK], v_ref[:, lanes(head)]) + dot_nn(
            raised[:, TOK:], v_all[0:TOK, lanes(head)]
        )

    pump(1)
    pump(2)

    absent = jnp.where((sec == 0) | (sec == 63), MASKED, 0.0)

    def pass_on(head):
        for d in range(2):
            source = lax.rem(x + (1 if d else 3), 4)
            here = gathered.at[source, :, lanes(head)]
            arrived(here, a_send.at[d, head], a_recv.at[d, head])
            half = gathered.at[source, pl.ds(d * (TOK // 2), TOK // 2), lanes(head)]
            send(half, half, f_send.at[d, head], f_recv.at[d, head], sec, x_left if d else x_right)

    for head in range(HEADS):
        arrived(
            k_all.at[by_far, lanes(head)], halo_send.at[4 + head], halo_recv.at[4 + head]
        )
        arrived(
            v_far.at[:, lanes(head)], halo_send.at[9 + head], halo_recv.at[9 + head]
        )
        scores = dot_nt(q_n[:, lanes(head)], k_all[2 * TOK :, lanes(head)]) + absent
        before = peak[head]
        highest = jnp.maximum(before[:, 0:1], jnp.max(scores, axis=-1, keepdims=True))
        raised = jnp.exp2(scores - highest)
        shrink = jnp.exp2(before - highest)
        sums = total[head] * shrink + jnp.sum(raised, axis=-1, keepdims=True)
        result = mixed[head] * shrink + dot_nn(
            raised.astype(jnp.bfloat16), v_all[TOK : 2 * TOK, lanes(head)]
        )
        gathered[x, :, lanes(head)] = (result / sums).astype(jnp.bfloat16)
        own = gathered.at[x, :, lanes(head)]
        for d in range(2):
            send(own, own, a_send.at[d, head], a_recv.at[d, head], sec, x_left if d else x_right)
        if head == 1:
            pump(3)
            pass_on(0)
        if head == 3:
            pump(4)
            pass_on(1)
    pass_on(2)
    pump(5)
    pump(6)
    pass_on(3)
    pass_on(4)
    pump(7)

    def project(half, piece, first_tile, tiles):
        own = half == h
        i = jnp.where(own, 1, 0)
        value = jnp.zeros((TOK, tiles * HD), jnp.float32)
        for block in range(4):
            start = block * 1280 + half * WIDTH + first_tile * HD
            value += dot_nt(
                gathered[block], weight[pl.ds(pl.multiple_of(start, HD), tiles * HD), :]
            )
        for t in range(tiles):
            part = value[:, lanes(t)]
            updated = (
                latent_ref[first_tile + t].astype(jnp.float32) + gate_ref[first_tile + t][0:1] * part
            )
            staged[i, first_tile + t] = jnp.where(own, updated, part).astype(jnp.bfloat16)
        send(
            staged.at[i, pl.ds(first_tile, tiles)],
            landed.at[i, pl.ds(first_tile, tiles)],
            o_send.at[i, piece],
            o_recv.at[i, piece],
            following,
            jnp.where(own, ten, other),
        )

    def project_side(shift):
        column = lax.rem(z + shift, 4)
        side = lax.rem(column, 2)
        project(lax.div(column, 2), 2 * side, 3 * side, 2)

    def project_middle(shift):
        project(lax.div(lax.rem(z + shift, 4), 2), 1, 2, 1)

    second_of_even(5)
    second_of_even(6)
    for k in range(7):
        twin_arrived(k)
    for head in range(HEADS):
        for d in range(2):
            half = gathered.at[lax.rem(x + 2, 4), pl.ds(d * (TOK // 2), TOK // 2), lanes(head)]
            arrived(half, f_send.at[d, head], f_recv.at[d, head])
    project_side(2)
    pump(8)
    second_of_even(7)
    twin_arrived(7)
    project_side(1)
    project_side(3)
    project_middle(2)
    second_of_even(8)
    twin_arrived(8)
    project_side(0)
    project_middle(0)

    ring_sent()
    for copy in sent:
        copy.wait_send()
    arrived(gate_prev, gate_send, gate_recv)
    for c, (start, size) in enumerate(PIECES):
        for i in range(2):
            arrived(landed.at[i, pl.ds(start, size)], o_send.at[i, c], o_recv.at[i, c])
        for t in range(start, start + size):
            out_ref[:, lanes(t)] = (
                landed[1, t].astype(jnp.float32)
                + gate_prev[t][0:1] * landed[0, t].astype(jnp.float32)
            ).astype(jnp.bfloat16)


def body(
    queries,
    keys,
    values,
    q_gain,
    k_gain,
    frame_offset,
    noise_level,
    gate_table,
    out_weight,
    latent,
    fresh,
):
    gains = jnp.stack([q_gain, k_gain])
    bf16, f32 = jnp.bfloat16, jnp.float32
    dma = pltpu.SemaphoreType.DMA
    moved = pl.pallas_call(
        kernel,
        out_shape=jax.ShapeDtypeStruct((TOK, WIDTH), bf16),
        in_specs=[pl.BlockSpec(memory_space=pltpu.SMEM)] * 2
        + [pl.BlockSpec(memory_space=pltpu.VMEM)]
        + [pl.BlockSpec(memory_space=pltpu.HBM)] * 6,
        out_specs=pl.BlockSpec(memory_space=pltpu.VMEM),
        scratch_shapes=[
            pltpu.VMEM((TOK, WIDTH), bf16),
            pltpu.VMEM((TOK, WIDTH), bf16),
            pltpu.VMEM((TOK, WIDTH), bf16),
            pltpu.VMEM((128, WIDTH), f32),
            pltpu.VMEM((HEADS, TOK, HD), bf16),
            pltpu.VMEM((HEADS, 8, HD), f32),
            dma((4 + HEADS,)),
            pltpu.VMEM((8, 8, TOK), f32),
            pltpu.VMEM((TOK, WIDTH), bf16),
            pltpu.VMEM((3 * TOK, WIDTH), bf16),
            pltpu.VMEM((2 * TOK, WIDTH), bf16),
            pltpu.VMEM((HEADS, TOK, HD), f32),
            pltpu.VMEM((HEADS, TOK, HD), f32),
            pltpu.VMEM((HEADS, TOK, HD), f32),
            pltpu.VMEM((4, TOK, WIDTH), bf16),
            pltpu.VMEM((D, WIDTH), bf16),
            pltpu.VMEM((2, HEADS, TOK, HD), bf16),
            pltpu.VMEM((2, HEADS, TOK, HD), bf16),
            pltpu.VMEM((HEADS, 8, HD), f32),
            dma((7,)),
            dma((7,)),
            dma((14,)),
            dma((14,)),
            dma,
            dma,
            dma,
            dma,
            dma,
            dma,
            dma((2, 15, len(PARTS))),
            dma((2, 15, len(PARTS))),
            dma((32,)),
            dma((32,)),
            dma((2, HEADS)),
            dma((2, HEADS)),
            dma((2, HEADS)),
            dma((2, HEADS)),
            dma((2, len(PIECES))),
            dma((2, len(PIECES))),
        ],
        compiler_params=pltpu.CompilerParams(
            collective_id=0, has_side_effects=True, vmem_limit_bytes=60 * 1024 * 1024
        ),
        cost_estimate=pl.CostEstimate(
            flops=3_700_000_000, bytes_accessed=4_000_000, transcendentals=2_300_000
        ),
    )(
        frame_offset, noise_level, gains, queries, keys, values, gate_table, latent, out_weight.T
    )
    return jnp.where(lax.axis_index("section") == 0, fresh, moved)


def solution(mesh):
    in_specs = (
        P("section", "tensor"),
        P("section", "tensor"),
        P("section", "tensor"),
        P("tensor"),
        P("tensor"),
        P("section"),
        P("section"),
        P(None, "tensor"),
        P("tensor", "section"),
        P("section", "tensor"),
        P(None, "tensor"),
    )
    out_specs = P("section", "tensor")
    return jax.shard_map(body, mesh=mesh, in_specs=in_specs, out_specs=out_specs, check_vma=False)
```
